32 devices in a mesh: groups: 2 (over y), atoms: 8 (over z, x), waves: 2 (over core).
Axes of the slice: x: 2, y: 2, z: 4, core: 2. Of those that a mesh axis runs over, the one named last changes fastest.
Arguments:
- features: bfloat16 [8192, 256], P(('groups', 'atoms', 'waves')), parts along dimension 0, may hold values from -6 to 6
- positions: float32 [3, 8192], P(None, ('groups', 'atoms', 'waves')), parts along dimension 1, may hold values from 0 to 1, as said below
- distances: float32 [8192, 768], P(('groups', 'atoms', 'waves')), parts along dimension 0, may hold values from 0.5 to 5
- pair_mask: int32 [8192, 768], P(('groups', 'atoms', 'waves')), parts along dimension 0, may hold values 0 or 1
- counts: int32 [32], P(('groups', 'atoms', 'waves')), parts along dimension 0, may hold values from 128 to 256, as said below
- wave_index: int32 [3, 2048], P(None, ('groups', 'waves')), parts along dimension 1, may hold values from -6 to 6
- w_value: bfloat16 [256, 256], replicated, may hold values from -0.375 to 0.375
- filter_short: float32 [16, 256], replicated, may hold values from -1 to 1
- filter_long: float32 [16, 256], replicated, may hold values from -6 to 6
- gain: float32 [256], replicated, may hold values from 0.1 to 1.9
- w_inner: bfloat16 [256, 256], replicated, may hold values from -0.375 to 0.375
- w_outer: bfloat16 [256, 256], replicated, may hold values from -0.375 to 0.375
Outputs:
- updated: bfloat16 [8192, 256], P(('groups', 'atoms', 'waves')), parts along dimension 0
The draws below stay inside these ranges and needn't reach their ends.
There are 2 independent parts, one for each index of `groups`. The reference program is written for one: setup_inputs(seed, part) draws one part's arguments, and reference() takes and returns one part's arrays. A program takes and returns all parts, laid end to end along the dimension named above; an argument that names none is the same for every part. Nothing has to cross between parts.
Inputs may be any that keep to these rules, and one draw needn't show every extreme that they name: The atoms of box b are its first counts[b] slots; in every draw some box is full. `positions`: fractional coordinates; the first coordinate of every slot of box b lies in [b / 16, (b + 1) / 16).
All inputs are finite; a program needn't handle non-finite values. No bound on the sum of `pair_mask` on one device may be relied on, other than what follows from the above.
Results may differ from the reference program's by a relative error of at most 0.015.
Values may be sent and summed in bfloat16 or wider, within the bound.
A program may use at most 64 MiB of HBM per device.

```python
import jax
import jax.numpy as jnp
from jax import lax

F = 256
NRBF = 16
ATOM_DEV = 256
BOXES = 16
ATOMS = 4096
KWAVES = 1024


def draw_positions(key, part):
    uniform = jax.random.uniform(key, (3, ATOMS), jnp.float32)
    box_of = (jnp.arange(ATOMS, dtype=jnp.int32) // ATOM_DEV).astype(jnp.float32)
    coord_first = (box_of + uniform[0]) / BOXES
    return jnp.stack([coord_first, uniform[1], uniform[2]]).astype(jnp.float32)


def draw_counts(key, part):
    keyone, keytwo = jax.random.split(jax.random.fold_in(key, 17))
    occupancy = jax.random.randint(keyone, (BOXES,), ATOM_DEV // 2, ATOM_DEV + 1)
    fullest = jax.random.randint(keytwo, (), 0, BOXES)
    return jnp.where(jnp.arange(BOXES, dtype=jnp.int32) == fullest, ATOM_DEV, occupancy).astype(jnp.int32)


def place_ends(values, own_key, smallest, largest):
    index_at = [jax.random.randint(jax.random.fold_in(own_key, axis), (), 0, length) for axis, length in enumerate(values.shape)]
    main_axis = values.shape.index(max(values.shape))
    neighbour = index_at[:main_axis] + [(index_at[main_axis] + 1) % values.shape[main_axis]] + index_at[main_axis + 1:]
    return values.at[tuple(index_at)].set(smallest).at[tuple(neighbour)].set(largest)


def block_levels(key, dims, cuts, low, top_value):
    factor_of = 1.0
    for position, parts in cuts:
        draws = jax.random.uniform(jax.random.fold_in(jax.random.fold_in(key, 6), position), (parts,), jnp.float32, low / len(cuts), top_value / len(cuts))
        factor_of = factor_of * jnp.repeat(jnp.exp(draws), dims[position] // parts).reshape((-1,) + (1,) * (len(dims) - 1 - position))
    return factor_of


def centred(rng, dims, scale, most, pieces=(), held_as=jnp.bfloat16):
    entries = scale * jax.random.normal(rng, dims, jnp.float32)
    if pieces:
        entries = entries * block_levels(rng, dims, pieces, -0.22, 0.18)
    return jnp.clip(entries, -most, most).astype(held_as)


def setup_inputs(seed: int = 0, part: int = 0) -> dict:
    key_of = jax.random.split(jax.random.key(seed), 13)
    part_keys = jax.random.split(jax.random.fold_in(key_of[12], part), 13)
    features = centred(part_keys[0], (ATOMS, F), 1.0, 6.0, ((0, 16),))
    positions = draw_positions(jax.random.fold_in(jax.random.fold_in(key_of[12], part), 71), part)
    distances = jnp.clip(0.5 + 4.5 * jax.random.uniform(part_keys[2], (ATOMS, 3 * ATOM_DEV), jnp.float32) ** block_levels(part_keys[2], (ATOMS, 3 * ATOM_DEV), ((0, 16),), -0.2, 0.2), 0.5, 5.0)
    pair_mask = place_ends((jax.random.randint(part_keys[3], (ATOMS, 3 * ATOM_DEV), 0, 2) < 1).astype(jnp.int32), jax.random.fold_in(part_keys[3], 1), 0, 1)
    counts = draw_counts(jax.random.fold_in(jax.random.fold_in(key_of[12], part), 71), part)
    wave_index = place_ends(jax.random.randint(part_keys[5], (3, KWAVES), -6, 7), jax.random.fold_in(part_keys[5], 1), -6, 6).astype(jnp.int32)
    w_value = centred(key_of[6], (F, F), F ** -0.5, 0.375)
    filter_short = centred(key_of[7], (NRBF, F), (ATOM_DEV ** -0.5), 1.0, (), jnp.float32)
    filter_long = centred(key_of[8], (NRBF, F), 2.0, 6.0, (), jnp.float32)
    gain = jnp.clip(1.0 + 0.18 * jax.random.normal(key_of[9], (F,), jnp.float32), 0.1, 1.9)
    w_inner = centred(key_of[10], (F, F), F ** -0.5, 0.375)
    w_outer = centred(key_of[11], (F, F), F ** -0.5, 0.375)
    return {"features": features, "positions": positions, "distances": distances, "pair_mask": pair_mask, "counts": counts, "wave_index": wave_index, "w_value": w_value, "filter_short": filter_short, "filter_long": filter_long, "gain": gain, "w_inner": w_inner, "w_outer": w_outer}


radius_cut = 5.0
wave_top = 6.0 * 3.0 ** 0.5

def radial_tiles(distances, pair_mask, radial_count):
    centres = radius_cut * jnp.arange(radial_count, dtype=jnp.float32) / (radial_count - 1)
    spacing = radius_cut / (radial_count - 1)
    envelope = 0.5 * (jnp.cos(jnp.pi * distances / radius_cut) + 1.0) * pair_mask.astype(jnp.float32)
    offsets = (distances[None] - centres[:, None, None]) / spacing
    tiles = jnp.exp(-0.5 * offsets * offsets) * envelope[None]
    return tiles.astype(jnp.bfloat16)

def phase_tiles(points, wave_index):
    waves = wave_index.astype(jnp.float32)
    theta = points[0][:, None] * waves[0][None, :] + points[1][:, None] * waves[1][None, :]
    theta = 2.0 * jnp.pi * (theta + points[2][:, None] * waves[2][None, :])
    return (jnp.cos(theta).astype(jnp.bfloat16), jnp.sin(theta).astype(jnp.bfloat16))

def wave_filter(wave_index, filter_long):
    waves = wave_index.astype(jnp.float32)
    radial_count = filter_long.shape[0]
    magnitude = jnp.sqrt(waves[0] * waves[0] + waves[1] * waves[1] + waves[2] * waves[2])
    centres = wave_top * jnp.arange(radial_count, dtype=jnp.float32) / (radial_count - 1)
    spacing = wave_top / (radial_count - 1)
    offsets = (magnitude[None, :] - centres[:, None]) / spacing
    k_basis = jnp.exp(-0.5 * offsets * offsets)
    return jnp.dot(k_basis.T, filter_long, precision=lax.Precision.HIGHEST)

def reference(features, positions, distances, pair_mask, counts, wave_index, w_value, filter_short, filter_long, gain, w_inner, w_outer):
    slot_index = jnp.arange(ATOMS, dtype=jnp.int32)
    occupied = (slot_index % ATOM_DEV < jnp.repeat(counts, ATOM_DEV)).astype(jnp.float32)
    values = (jnp.dot(features, w_value, preferred_element_type=jnp.float32) * occupied[:, None]).astype(jnp.bfloat16)
    extended = jnp.concatenate([values[ATOMS - ATOM_DEV:], values, values[:ATOM_DEV]], 0)

    def near_box(box):
        begin = (box * ATOM_DEV).astype(jnp.int32)
        beside_all = lax.dynamic_slice_in_dim(extended, begin, 3 * ATOM_DEV, 0)
        box_dist = lax.dynamic_slice_in_dim(distances, begin, ATOM_DEV, 0)
        box_mask = lax.dynamic_slice_in_dim(pair_mask, begin, ATOM_DEV, 0)
        tiles = radial_tiles(box_dist, box_mask, NRBF).reshape(NRBF * ATOM_DEV, 3 * ATOM_DEV)
        products = jnp.dot(tiles.astype(jnp.float32), beside_all.astype(jnp.float32), precision=lax.Precision.HIGHEST)
        products = products.reshape(NRBF, ATOM_DEV, F)
        return lax.optimization_barrier(jnp.sum(products * filter_short[:, None, :], axis=0))
    near_field = lax.map(near_box, jnp.arange(BOXES, dtype=jnp.int32)).reshape(ATOMS, F)
    block = 2 * ATOM_DEV
    block_ids = jnp.arange(ATOMS // block, dtype=jnp.int32)

    def add_factors(carry, index):
        begin = (index * block).astype(jnp.int32)
        points = lax.dynamic_slice_in_dim(positions, begin, block, 1)
        block_values = lax.dynamic_slice_in_dim(values, begin, block, 0)
        cosine, sine = phase_tiles(points, wave_index)
        cos_acc = carry[0] + jnp.dot(cosine.T, block_values, preferred_element_type=jnp.float32)
        sin_acc = carry[1] + jnp.dot(sine.T, block_values, preferred_element_type=jnp.float32)
        return ((cos_acc, sin_acc), None)
    zeros = jnp.zeros((KWAVES, F), jnp.float32)
    (cos_sum, sin_sum), unused = lax.scan(add_factors, (zeros, zeros), block_ids)
    filt = wave_filter(wave_index, filter_long)
    factor_scale = float(ATOMS) ** (-0.5)
    cos_filtered = (cos_sum * filt * factor_scale).astype(jnp.bfloat16)
    sin_filtered = (sin_sum * filt * factor_scale).astype(jnp.bfloat16)

    def far_block(index):
        begin = (index * block).astype(jnp.int32)
        points = lax.dynamic_slice_in_dim(positions, begin, block, 1)
        cosine, sine = phase_tiles(points, wave_index)
        summed = jnp.dot(cosine, cos_filtered, preferred_element_type=jnp.float32) + jnp.dot(sine, sin_filtered, preferred_element_type=jnp.float32)
        return summed * float(KWAVES) ** (-0.5)
    far_field = lax.map(far_block, block_ids).reshape(ATOMS, F)
    combined = features.astype(jnp.float32) + near_field + far_field
    normed = (combined * lax.rsqrt(lax.optimization_barrier(jnp.mean(combined * combined, axis=-1, keepdims=True)) + 1e-06) * gain).astype(jnp.bfloat16)
    inner = jax.nn.silu(jnp.dot(normed, w_inner, preferred_element_type=jnp.float32)).astype(jnp.bfloat16)
    result = jnp.dot(inner, w_outer, preferred_element_type=jnp.float32) * occupied[:, None]
    return result.astype(jnp.bfloat16)
```

```python
import functools
import math

import jax
import jax.numpy as jnp
from jax import lax
from jax.experimental import pallas as pl
from jax.experimental.pallas import tpu as pltpu
from jax.sharding import PartitionSpec as P

radius_cut = 5.0
wave_top = 6.0 * 3.0**0.5


def padded(block, sides, width):
    for axis, dim in sides:
        count = lax.axis_size(axis)
        forward = [(i, i + 1) for i in range(count - 1)]
        forward.append((count - 1, 0))
        backward = [(target, source) for source, target in forward]
        low = lax.ppermute(
            lax.slice_in_dim(block, block.shape[dim] - width, None, axis=dim), axis, forward
        )
        high = lax.ppermute(lax.slice_in_dim(block, 0, width, axis=dim), axis, backward)
        block = jnp.concatenate([low, block, high], axis=dim)
    return block


def radial_tiles(distances, pair_mask, radial_count):
    centres = radius_cut * jnp.arange(radial_count, dtype=jnp.float32) / (radial_count - 1)
    spacing = radius_cut / (radial_count - 1)
    envelope = (
        0.5 * (jnp.cos(jnp.pi * distances / radius_cut) + 1.0) * pair_mask.astype(jnp.float32)
    )
    offsets = (distances[None] - centres[:, None, None]) / spacing
    tiles = jnp.exp(-0.5 * offsets * offsets) * envelope[None]
    return tiles.astype(jnp.bfloat16)


def phase_tiles(points, wave_index):
    waves = wave_index.astype(jnp.float32)
    theta = points[0][:, None] * waves[0][None, :] + points[1][:, None] * waves[1][None, :]
    theta = 2.0 * jnp.pi * (theta + points[2][:, None] * waves[2][None, :])
    return (jnp.cos(theta).astype(jnp.bfloat16), jnp.sin(theta).astype(jnp.bfloat16))


def wave_filter(wave_index, filter_long):
    waves = wave_index.astype(jnp.float32)
    radial_count = filter_long.shape[0]
    magnitude = jnp.sqrt(waves[0] * waves[0] + waves[1] * waves[1] + waves[2] * waves[2])
    centres = wave_top * jnp.arange(radial_count, dtype=jnp.float32) / (radial_count - 1)
    spacing = wave_top / (radial_count - 1)
    offsets = (magnitude[None, :] - centres[:, None]) / spacing
    k_basis = jnp.exp(-0.5 * offsets * offsets)
    return jnp.dot(k_basis.T, filter_long, precision=lax.Precision.HIGHEST)


def collective_body(
    features,
    positions,
    distances,
    pair_mask,
    counts,
    wave_index,
    w_value,
    filter_short,
    filter_long,
    gain,
    w_inner,
    w_outer,
):
    row_count = features.shape[0]
    width = features.shape[1]
    radial_count = filter_short.shape[0]
    occupied = (lax.iota(jnp.int32, row_count) < counts[0]).astype(jnp.float32)
    values = (
        jnp.dot(features, w_value, preferred_element_type=jnp.float32) * occupied[:, None]
    ).astype(jnp.bfloat16)
    beside_all = padded(values, ((("atoms", "waves"), 0),), row_count)
    tiles = radial_tiles(distances, pair_mask, radial_count).reshape(
        radial_count * row_count, 3 * row_count
    )
    products = jnp.dot(tiles, beside_all, preferred_element_type=jnp.float32).reshape(
        radial_count, row_count, width
    )
    near_field = jnp.sum(products * filter_short[:, None, :], axis=0)
    wide_values, block_points = (
        lax.all_gather(values.astype(jnp.float32), "waves", axis=0, tiled=True),
        lax.all_gather(positions, "waves", axis=1, tiled=True),
    )
    block_values = wide_values.astype(jnp.bfloat16)
    cosine, sine = phase_tiles(block_points, wave_index)
    cos_sum = jnp.einsum("ak,af->kf", cosine, block_values, preferred_element_type=jnp.float32)
    sin_sum = jnp.einsum("ak,af->kf", sine, block_values, preferred_element_type=jnp.float32)
    atom_total = row_count * lax.axis_size(("atoms", "waves"))
    wave_total = wave_index.shape[1] * lax.axis_size("waves")
    factor_scale = float(atom_total) ** (-0.5)
    cos_total, sin_total = lax.psum((cos_sum, sin_sum), "atoms")
    block_filter = wave_filter(wave_index, filter_long)
    cos_filtered = (cos_total * block_filter * factor_scale).astype(jnp.bfloat16)
    sin_filtered = (sin_total * block_filter * factor_scale).astype(jnp.bfloat16)
    far_field = lax.psum_scatter(
        (
            jnp.dot(cosine, cos_filtered, preferred_element_type=jnp.float32)
            + jnp.dot(sine, sin_filtered, preferred_element_type=jnp.float32)
        ).astype(jnp.bfloat16),
        "waves",
        scatter_dimension=0,
        tiled=True,
    ).astype(jnp.float32) * float(wave_total) ** (-0.5)
    combined = features.astype(jnp.float32) + near_field + far_field
    normed = (
        combined * lax.rsqrt(jnp.mean(combined * combined, axis=-1, keepdims=True) + 1e-06) * gain
    ).astype(jnp.bfloat16)
    inner = jax.nn.silu(jnp.dot(normed, w_inner, preferred_element_type=jnp.float32)).astype(
        jnp.bfloat16
    )
    result = jnp.dot(inner, w_outer, preferred_element_type=jnp.float32) * occupied[:, None]
    return result.astype(jnp.bfloat16)


MESH = pl.DeviceIdType.MESH
cos_terms = (
    0.9999999890590217,
    -19.73920449945381,
    64.93911745989173,
    -85.45013953082398,
    60.16763095051855,
    -25.967599246994247,
    6.528658159389057,
)
sin_terms = (
    6.283184916495431,
    -41.34158923268848,
    81.59994332978006,
    -76.61447253122435,
    41.34288235446963,
    -12.471243534886277,
)


def horner(square, terms):
    total = square * terms[-1] + terms[-2]
    for term in terms[-3::-1]:
        total = total * square + term
    return total


def turned(turns):
    part = turns - jnp.floor(turns + 0.5)
    square = part * part
    return horner(square, cos_terms), part * horner(square, sin_terms)


def split_of(count):
    low = 1
    for size in range(1, count + 1):
        if count % size == 0 and size * size <= count:
            low = size
    return low, count // low


def kernel(
    low_count,
    high_count,
    features,
    positions,
    distances,
    pair_mask,
    counts,
    wave_index,
    w_value,
    filter_short,
    filter_long,
    gain,
    w_inner,
    w_outer,
    updated,
    dist,
    mask,
    values,
    points,
    waves,
    wave_cols,
    phases,
    phases_t,
    own_sums,
    low_out,
    low_in,
    high_out,
    high_in,
    filtered,
    block_filter,
    envelope,
    tiles,
    near,
    far_out,
    far_in,
    load_sem,
    pair_send,
    pair_recv,
    low_send,
    low_recv,
    high_send,
    high_recv,
    spread_send,
    spread_recv,
    relay_send,
    relay_recv,
):
    rows = features.shape[0]
    radial_count = filter_short.shape[0]
    wave_count = wave_index.shape[1]
    atoms_count = low_count * high_count
    chunk = wave_count // atoms_count
    a = lax.axis_index("atoms")
    w = lax.axis_index("waves")
    high, low = a // low_count, a % low_count
    partner = {"atoms": a, "waves": 1 - w}
    other = {"atoms": (a + 2 * w - 1 + atoms_count) % atoms_count, "waves": 1 - w}

    def low_peer(step):
        return {"atoms": high * low_count + (low + step) % low_count, "waves": w}

    def high_peer(step):
        return {"atoms": ((high + step) % high_count) * low_count + low, "waves": w}

    peers = [partner, other]
    peers += [low_peer(step) for step in range(1, low_count)]
    peers += [high_peer(step) for step in range(1, high_count)]

    load_dist = pltpu.make_async_copy(distances, dist, load_sem.at[0])
    load_mask = pltpu.make_async_copy(pair_mask, mask, load_sem.at[1])
    load_dist.start()
    load_mask.start()
    barrier = pltpu.get_barrier_semaphore()
    for peer in peers:
        pl.semaphore_signal(barrier, inc=1, device_id=peer, device_id_type=MESH)

    def remote(src, dst, send, recv, peer):
        copy = pltpu.make_async_remote_copy(
            src_ref=src,
            dst_ref=dst,
            send_sem=send,
            recv_sem=recv,
            device_id=peer,
            device_id_type=MESH,
        )
        copy.start()
        return copy

    occupied = (lax.broadcasted_iota(jnp.int32, (rows, 1), 0) < counts[0]).astype(jnp.float32)
    values[1] = (
        jnp.dot(features[...], w_value[...], preferred_element_type=jnp.float32) * occupied
    ).astype(jnp.bfloat16)
    points[0] = positions[...]
    waves[...] = jnp.zeros_like(waves)
    waves[0:3, :] = wave_index[...].astype(jnp.float32)
    pl.semaphore_wait(barrier, len(peers))

    started = []
    points_copy = remote(points.at[0], points.at[1], pair_send.at[0], pair_recv.at[0], partner)
    pair_copy = remote(
        values.at[1], values.at[2 * w], pair_send.at[1], pair_recv.at[1], partner
    )
    other_copy = remote(
        values.at[1], values.at[2 - 2 * w], pair_send.at[2], pair_recv.at[2], other
    )
    started += [points_copy, pair_copy, other_copy]

    wave = waves[...]
    magnitude = jnp.sqrt(
        wave[0:1] * wave[0:1] + wave[1:2] * wave[1:2] + wave[2:3] * wave[2:3]
    )
    spacing = wave_top / (radial_count - 1)
    centres = lax.broadcasted_iota(jnp.int32, (radial_count, 1), 0).astype(jnp.float32) * spacing
    offsets = (magnitude - centres) / spacing
    k_basis = jnp.exp(-0.5 * offsets * offsets)
    block_filter[...] = lax.dot_general(
        k_basis,
        filter_long[...],
        (((0,), (0,)), ((), ())),
        precision=lax.Precision.HIGHEST,
        preferred_element_type=jnp.float32,
    ) * (float(rows * 2 * atoms_count) ** -0.5)
    wave_t = wave.T

    points_copy.wait_recv()
    point_rows = jnp.concatenate([points[0], points[1]], axis=1)

    order = sorted(range(high_count), key=lambda e: (e == 0, abs(2 * e - high_count)))

    wave_cols[...] = wave_t

    def chunk_sums(index):
        begin = pl.multiple_of(index * chunk, chunk)
        base = pl.multiple_of(index * 2 * chunk, 2 * chunk)
        cols = wave_cols[pl.ds(begin, chunk), :]
        turns = cols[:, 0:1] * point_rows[0:1] + cols[:, 1:2] * point_rows[1:2]
        turns = turns + cols[:, 2:3] * point_rows[2:3]
        cosine, sine = turned(turns)
        phases[pl.ds(base, chunk), :] = cosine.astype(jnp.bfloat16)
        phases[pl.ds(base + chunk, chunk), :] = sine.astype(jnp.bfloat16)
        block = phases[pl.ds(base, 2 * chunk), :]
        return jnp.dot(
            block[:, 0:rows], values[1], preferred_element_type=jnp.float32
        ) + jnp.dot(
            block[:, rows : 2 * rows], values[2 - 2 * w], preferred_element_type=jnp.float32
        )

    first = True
    low_copies = {}
    for step in range(1, low_count):
        for e in order:
            index = ((high + e) % high_count) * low_count + (low + step) % low_count
            if first:
                pair_copy.wait_recv()
                first = False
            low_out[step - 1, e] = chunk_sums(index).astype(jnp.bfloat16)
            low_copies[step, e] = remote(
                low_out.at[step - 1, e],
                low_in.at[step - 1, e],
                low_send.at[step - 1, e],
                low_recv.at[step - 1, e],
                low_peer(step),
            )
            started.append(low_copies[step, e])
    for e in order:
        own_sums[e] = chunk_sums(((high + e) % high_count) * low_count + low)

    load_dist.wait()
    load_mask.wait()
    turns = dist[...] * (0.5 / radius_cut)
    part = turns - jnp.floor(turns + 0.5)
    envelope[...] = (0.5 * horner(part * part, cos_terms) + 0.5) * mask[...].astype(jnp.float32)
    near[...] = jnp.zeros_like(near)
    other_copy.wait_recv()
    sharp = math.sqrt(0.5 * math.log2(math.e)) * (radial_count - 1) / radius_cut
    shift = radius_cut / (radial_count - 1)

    def near_pair(k2, carry):
        for half in range(2):
            k = k2 * 2 + half
            offset = (dist[...] - k.astype(jnp.float32) * shift) * sharp
            tiles[half * rows : (half + 1) * rows, :] = (
                jnp.exp2(-(offset * offset)) * envelope[...]
            ).astype(jnp.bfloat16)
        beside = values[...].reshape(3 * rows, values.shape[2])
        products = jnp.dot(tiles[...], beside, preferred_element_type=jnp.float32)
        near[...] += (
            products[0:rows] * filter_short[pl.ds(k2 * 2, 1), :]
            + products[rows : 2 * rows] * filter_short[pl.ds(k2 * 2 + 1, 1), :]
        )
        return carry

    pairs = radial_count // 2
    done = 0

    def near_until(stop):
        nonlocal done
        if stop > done:
            lax.fori_loop(done, stop, near_pair, 0)
            done = stop

    high_copies = {}
    for place, e in enumerate(order):
        near_until(min(pairs, place + 1))
        total = own_sums[e]
        for step in range(1, low_count):
            low_copies[step, e].wait_recv()
            total = total + low_in[step - 1, e].astype(jnp.float32)
        if e == 0:
            own_sums[0] = total
        else:
            high_out[e - 1] = total.astype(jnp.bfloat16)
            high_copies[e] = remote(
                high_out.at[e - 1],
                high_in.at[e - 1],
                high_send.at[e - 1],
                high_recv.at[e - 1],
                high_peer(e),
            )
            started.append(high_copies[e])

    near_until(min(pairs, high_count + 2))
    total = own_sums[0]
    for e in range(1, high_count):
        high_copies[e].wait_recv()
        total = total + high_in[e - 1].astype(jnp.float32)
    own_filter = block_filter[pl.ds(pl.multiple_of(a * chunk, chunk), chunk), :]

    def chunk_rows(index):
        return pl.ds(pl.multiple_of(index * 2 * chunk, 2 * chunk), 2 * chunk)

    own_rows = chunk_rows(a)
    filtered[own_rows, :] = (total * jnp.concatenate([own_filter, own_filter], axis=0)).astype(
        jnp.bfloat16
    )
    spread = {}
    for e in order:
        if e:
            spread[e] = remote(
                filtered.at[own_rows],
                filtered.at[own_rows],
                spread_send.at[e - 1],
                spread_recv.at[e - 1],
                high_peer(e),
            )
            started.append(spread[e])
    relay = []

    def pass_on(e):
        source = ((high - e + high_count) % high_count) * low_count + low
        for step in range(1, low_count):
            copy = remote(
                filtered.at[chunk_rows(source)],
                filtered.at[chunk_rows(source)],
                relay_send.at[step - 1, e],
                relay_recv.at[step - 1, e],
                low_peer(step),
            )
            relay.append(copy)
            started.append(copy)

    pass_on(0)
    near_until(pairs)
    phases_t[...] = phases[...].T
    for e in sorted(range(1, high_count), key=lambda e: -abs(2 * e - high_count)):
        spread[e].wait_recv()
        pass_on(e)
    for copy in relay:
        copy.wait_recv()

    far_out[...] = jnp.dot(
        phases_t[rows : 2 * rows, :], filtered[...], preferred_element_type=jnp.float32
    ).astype(jnp.bfloat16)
    far_copy = remote(far_out, far_in, pair_send.at[3], pair_recv.at[3], partner)
    started.append(far_copy)
    own_far = jnp.dot(phases_t[0:rows, :], filtered[...], preferred_element_type=jnp.float32)
    combined = features[...].astype(jnp.float32) + near[...]
    far_copy.wait_recv()
    far_field = (own_far + far_in[...].astype(jnp.float32)) * (float(2 * wave_count) ** -0.5)
    combined = combined + far_field
    normed = (
        combined
        * lax.rsqrt(jnp.mean(combined * combined, axis=-1, keepdims=True) + 1e-06)
        * gain[...]
    ).astype(jnp.bfloat16)
    inner = jnp.dot(normed, w_inner[...], preferred_element_type=jnp.float32)
    inner = (inner / (1.0 + jnp.exp(-inner))).astype(jnp.bfloat16)
    result = jnp.dot(inner, w_outer[...], preferred_element_type=jnp.float32) * occupied
    updated[...] = result.astype(jnp.bfloat16)
    for copy in started:
        copy.wait_send()


def kernel_body(low_count, high_count, features, positions, distances, pair_mask, counts,
                wave_index, w_value, filter_short, filter_long, gain, w_inner, w_outer):
    rows, width = features.shape
    wave_count = wave_index.shape[1]
    atoms_count = low_count * high_count
    chunk2 = 2 * wave_count // atoms_count
    columns = distances.shape[1]
    bf16, f32 = jnp.bfloat16, jnp.float32
    vmem = pl.BlockSpec(memory_space=pltpu.VMEM)
    hbm = pl.BlockSpec(memory_space=pl.ANY)
    smem = pl.BlockSpec(memory_space=pltpu.SMEM)
    dma = pltpu.SemaphoreType.DMA
    return pl.pallas_call(
        functools.partial(kernel, low_count, high_count),
        out_shape=jax.ShapeDtypeStruct((rows, width), bf16),
        in_specs=[vmem, vmem, hbm, hbm, smem] + [vmem] * 7,
        out_specs=vmem,
        scratch_shapes=[
            pltpu.VMEM((rows, columns), f32),
            pltpu.VMEM((rows, columns), jnp.int32),
            pltpu.VMEM((3, rows, width), bf16),
            pltpu.VMEM((2, 3, rows), f32),
            pltpu.VMEM((8, wave_count), f32),
            pltpu.VMEM((wave_count, 8), f32),
            pltpu.VMEM((2 * wave_count, 2 * rows), bf16),
            pltpu.VMEM((2 * rows, 2 * wave_count), bf16),
            pltpu.VMEM((high_count, chunk2, width), f32),
            pltpu.VMEM((low_count - 1, high_count, chunk2, width), bf16),
            pltpu.VMEM((low_count - 1, high_count, chunk2, width), bf16),
            pltpu.VMEM((high_count - 1, chunk2, width), bf16),
            pltpu.VMEM((high_count - 1, chunk2, width), bf16),
            pltpu.VMEM((2 * wave_count, width), bf16),
            pltpu.VMEM((wave_count, width), f32),
            pltpu.VMEM((rows, columns), f32),
            pltpu.VMEM((2 * rows, columns), bf16),
            pltpu.VMEM((rows, width), f32),
            pltpu.VMEM((rows, width), bf16),
            pltpu.VMEM((rows, width), bf16),
            dma((2,)),
            dma((4,)),
            dma((4,)),
            dma((low_count - 1, high_count)),
            dma((low_count - 1, high_count)),
            dma((high_count - 1,)),
            dma((high_count - 1,)),
            dma((high_count - 1,)),
            dma((high_count - 1,)),
            dma((low_count - 1, high_count)),
            dma((low_count - 1, high_count)),
        ],
        compiler_params=pltpu.CompilerParams(
            collective_id=0, has_side_effects=True, vmem_limit_bytes=40 * 1024 * 1024
        ),
        cost_estimate=pl.CostEstimate(
            flops=2 * rows * columns * width * filter_short.shape[0],
            bytes_accessed=8 * rows * columns,
            transcendentals=rows * columns * filter_short.shape[0],
        ),
    )(features, positions, distances, pair_mask, counts, wave_index, w_value, filter_short,
      filter_long, gain.reshape(1, width), w_inner, w_outer)


def body_for(mesh):
    atoms_count = mesh.shape["atoms"]
    low_count, high_count = split_of(atoms_count)

    def body(*arrays):
        chunk = arrays[5].shape[1] // atoms_count
        if low_count > 1 and chunk % 16 == 0 and arrays[5].shape[1] % atoms_count == 0:
            return kernel_body(low_count, high_count, *arrays)
        return collective_body(*arrays)

    return body


def solution(mesh):
    placed = (
        P(("groups", "atoms", "waves"), None),
        P(None, ("groups", "atoms", "waves")),
        P(("groups", "atoms", "waves"), None),
        P(("groups", "atoms", "waves"), None),
        P(("groups", "atoms", "waves")),
        P(None, ("groups", "waves")),
        P(),
        P(),
        P(),
        P(),
        P(),
        P(),
    )
    return jax.shard_map(
        body_for(mesh),
        mesh=mesh,
        in_specs=placed,
        out_specs=P(("groups", "atoms", "waves"), None),
        check_vma=False,
    )
```

```python
import functools
import math

import jax
import jax.numpy as jnp
from jax import lax
from jax.experimental import pallas as pl
from jax.experimental.pallas import tpu as pltpu
from jax.sharding import PartitionSpec as P

radius_cut = 5.0
wave_top = 6.0 * 3.0**0.5


def padded(block, sides, width):
    for axis, dim in sides:
        count = lax.axis_size(axis)
        forward = [(i, i + 1) for i in range(count - 1)]
        forward.append((count - 1, 0))
        backward = [(target, source) for source, target in forward]
        low = lax.ppermute(
            lax.slice_in_dim(block, block.shape[dim] - width, None, axis=dim), axis, forward
        )
        high = lax.ppermute(lax.slice_in_dim(block, 0, width, axis=dim), axis, backward)
        block = jnp.concatenate([low, block, high], axis=dim)
    return block


def radial_tiles(distances, pair_mask, radial_count):
    centres = radius_cut * jnp.arange(radial_count, dtype=jnp.float32) / (radial_count - 1)
    spacing = radius_cut / (radial_count - 1)
    envelope = (
        0.5 * (jnp.cos(jnp.pi * distances / radius_cut) + 1.0) * pair_mask.astype(jnp.float32)
    )
    offsets = (distances[None] - centres[:, None, None]) / spacing
    tiles = jnp.exp(-0.5 * offsets * offsets) * envelope[None]
    return tiles.astype(jnp.bfloat16)


def phase_tiles(points, wave_index):
    waves = wave_index.astype(jnp.float32)
    theta = points[0][:, None] * waves[0][None, :] + points[1][:, None] * waves[1][None, :]
    theta = 2.0 * jnp.pi * (theta + points[2][:, None] * waves[2][None, :])
    return (jnp.cos(theta).astype(jnp.bfloat16), jnp.sin(theta).astype(jnp.bfloat16))


def wave_filter(wave_index, filter_long):
    waves = wave_index.astype(jnp.float32)
    radial_count = filter_long.shape[0]
    magnitude = jnp.sqrt(waves[0] * waves[0] + waves[1] * waves[1] + waves[2] * waves[2])
    centres = wave_top * jnp.arange(radial_count, dtype=jnp.float32) / (radial_count - 1)
    spacing = wave_top / (radial_count - 1)
    offsets = (magnitude[None, :] - centres[:, None]) / spacing
    k_basis = jnp.exp(-0.5 * offsets * offsets)
    return jnp.dot(k_basis.T, filter_long, precision=lax.Precision.HIGHEST)


def collective_body(
    features,
    positions,
    distances,
    pair_mask,
    counts,
    wave_index,
    w_value,
    filter_short,
    filter_long,
    gain,
    w_inner,
    w_outer,
):
    row_count = features.shape[0]
    width = features.shape[1]
    radial_count = filter_short.shape[0]
    occupied = (lax.iota(jnp.int32, row_count) < counts[0]).astype(jnp.float32)
    values = (
        jnp.dot(features, w_value, preferred_element_type=jnp.float32) * occupied[:, None]
    ).astype(jnp.bfloat16)
    beside_all = padded(values, ((("atoms", "waves"), 0),), row_count)
    tiles = radial_tiles(distances, pair_mask, radial_count).reshape(
        radial_count * row_count, 3 * row_count
    )
    products = jnp.dot(tiles, beside_all, preferred_element_type=jnp.float32).reshape(
        radial_count, row_count, width
    )
    near_field = jnp.sum(products * filter_short[:, None, :], axis=0)
    wide_values, block_points = (
        lax.all_gather(values.astype(jnp.float32), "waves", axis=0, tiled=True),
        lax.all_gather(positions, "waves", axis=1, tiled=True),
    )
    block_values = wide_values.astype(jnp.bfloat16)
    cosine, sine = phase_tiles(block_points, wave_index)
    cos_sum = jnp.einsum("ak,af->kf", cosine, block_values, preferred_element_type=jnp.float32)
    sin_sum = jnp.einsum("ak,af->kf", sine, block_values, preferred_element_type=jnp.float32)
    atom_total = row_count * lax.axis_size(("atoms", "waves"))
    wave_total = wave_index.shape[1] * lax.axis_size("waves")
    factor_scale = float(atom_total) ** (-0.5)
    cos_total, sin_total = lax.psum((cos_sum, sin_sum), "atoms")
    block_filter = wave_filter(wave_index, filter_long)
    cos_filtered = (cos_total * block_filter * factor_scale).astype(jnp.bfloat16)
    sin_filtered = (sin_total * block_filter * factor_scale).astype(jnp.bfloat16)
    far_field = lax.psum_scatter(
        (
            jnp.dot(cosine, cos_filtered, preferred_element_type=jnp.float32)
            + jnp.dot(sine, sin_filtered, preferred_element_type=jnp.float32)
        ).astype(jnp.bfloat16),
        "waves",
        scatter_dimension=0,
        tiled=True,
    ).astype(jnp.float32) * float(wave_total) ** (-0.5)
    combined = features.astype(jnp.float32) + near_field + far_field
    normed = (
        combined * lax.rsqrt(jnp.mean(combined * combined, axis=-1, keepdims=True) + 1e-06) * gain
    ).astype(jnp.bfloat16)
    inner = jax.nn.silu(jnp.dot(normed, w_inner, preferred_element_type=jnp.float32)).astype(
        jnp.bfloat16
    )
    result = jnp.dot(inner, w_outer, preferred_element_type=jnp.float32) * occupied[:, None]
    return result.astype(jnp.bfloat16)


MESH = pl.DeviceIdType.MESH
cos_terms = (
    0.9999999890590217,
    -19.73920449945381,
    64.93911745989173,
    -85.45013953082398,
    60.16763095051855,
    -25.967599246994247,
    6.528658159389057,
)
sin_terms = (
    6.283184916495431,
    -41.34158923268848,
    81.59994332978006,
    -76.61447253122435,
    41.34288235446963,
    -12.471243534886277,
)


def horner(square, terms):
    total = square * terms[-1] + terms[-2]
    for term in terms[-3::-1]:
        total = total * square + term
    return total


def turned(turns):
    part = turns - jnp.floor(turns + 0.5)
    square = part * part
    return horner(square, cos_terms), part * horner(square, sin_terms)


def split_of(count):
    low = 1
    for size in range(1, count + 1):
        if count % size == 0 and size * size <= count:
            low = size
    return low, count // low


def kernel(
    low_count,
    high_count,
    features_hbm,
    positions_hbm,
    distances_hbm,
    pair_mask_hbm,
    counts,
    wave_index_hbm,
    w_value_hbm,
    filter_short_hbm,
    filter_long_hbm,
    gain_hbm,
    w_inner_hbm,
    w_outer_hbm,
    updated,
    features,
    dist,
    mask,
    wave_index,
    w_value,
    filter_short,
    filter_long,
    gain,
    w_inner,
    w_outer,
    values,
    points,
    waves,
    wave_cols,
    phases,
    phases_t,
    own_sums,
    low_out,
    low_in,
    high_out,
    high_in,
    filtered,
    block_filter,
    envelope,
    tiles,
    near,
    far_out,
    far_in,
    load_sem,
    pair_send,
    pair_recv,
    low_send,
    low_recv,
    high_send,
    high_recv,
    spread_send,
    spread_recv,
    relay_send,
    relay_recv,
):
    rows = features.shape[0]
    radial_count = filter_short.shape[0]
    wave_count = wave_index.shape[1]
    atoms_count = low_count * high_count
    chunk = wave_count // atoms_count
    a = lax.axis_index("atoms")
    w = lax.axis_index("waves")
    high, low = a // low_count, a % low_count
    partner = {"atoms": a, "waves": 1 - w}
    other = {"atoms": (a + 2 * w - 1 + atoms_count) % atoms_count, "waves": 1 - w}

    def low_peer(step):
        return {"atoms": high * low_count + (low + step) % low_count, "waves": w}

    def high_peer(step):
        return {"atoms": ((high + step) % high_count) * low_count + low, "waves": w}

    peers = [partner, other]
    peers += [low_peer(step) for step in range(1, low_count)]
    peers += [high_peer(step) for step in range(1, high_count)]

    sources = (
        (features_hbm, features),
        (w_value_hbm, w_value),
        (positions_hbm, points.at[0]),
        (wave_index_hbm, wave_index),
        (filter_long_hbm, filter_long),
        (distances_hbm, dist),
        (pair_mask_hbm, mask),
        (filter_short_hbm, filter_short),
        (gain_hbm, gain),
        (w_inner_hbm, w_inner),
        (w_outer_hbm, w_outer),
    )
    loads = [
        pltpu.make_async_copy(source, target, load_sem.at[place])
        for place, (source, target) in enumerate(sources)
    ]
    barrier = pltpu.get_barrier_semaphore()
    for peer in peers:
        pl.semaphore_signal(barrier, inc=1, device_id=peer, device_id_type=MESH)
    for load in loads:
        load.start()

    def remote(src, dst, send, recv, peer):
        copy = pltpu.make_async_remote_copy(
            src_ref=src,
            dst_ref=dst,
            send_sem=send,
            recv_sem=recv,
            device_id=peer,
            device_id_type=MESH,
        )
        copy.start()
        return copy

    for load in loads[:4]:
        load.wait()
    occupied = (lax.broadcasted_iota(jnp.int32, (rows, 1), 0) < counts[0]).astype(jnp.float32)
    values[1] = (
        jnp.dot(features[...], w_value[...], preferred_element_type=jnp.float32) * occupied
    ).astype(jnp.bfloat16)
    waves[...] = jnp.zeros_like(waves)
    waves[0:3, :] = wave_index[...].astype(jnp.float32)
    pl.semaphore_wait(barrier, len(peers))

    started = []
    points_copy = remote(points.at[0], points.at[1], pair_send.at[0], pair_recv.at[0], partner)
    pair_copy = remote(
        values.at[1], values.at[2 * w], pair_send.at[1], pair_recv.at[1], partner
    )
    other_copy = remote(
        values.at[1], values.at[2 - 2 * w], pair_send.at[2], pair_recv.at[2], other
    )
    started += [points_copy, pair_copy, other_copy]

    loads[4].wait()
    wave = waves[...]
    magnitude = jnp.sqrt(
        wave[0:1] * wave[0:1] + wave[1:2] * wave[1:2] + wave[2:3] * wave[2:3]
    )
    spacing = wave_top / (radial_count - 1)
    centres = lax.broadcasted_iota(jnp.int32, (radial_count, 1), 0).astype(jnp.float32) * spacing
    offsets = (magnitude - centres) / spacing
    k_basis = jnp.exp(-0.5 * offsets * offsets)
    block_filter[...] = lax.dot_general(
        k_basis,
        filter_long[...],
        (((0,), (0,)), ((), ())),
        precision=lax.Precision.HIGHEST,
        preferred_element_type=jnp.float32,
    ) * (float(rows * 2 * atoms_count) ** -0.5)
    wave_t = wave.T

    points_copy.wait_recv()
    point_rows = jnp.concatenate([points[0], points[1]], axis=1)

    order = sorted(range(high_count), key=lambda e: (e == 0, abs(2 * e - high_count)))

    wave_cols[...] = wave_t

    def chunk_sums(index):
        begin = pl.multiple_of(index * chunk, chunk)
        base = pl.multiple_of(index * 2 * chunk, 2 * chunk)
        cols = wave_cols[pl.ds(begin, chunk), :]
        turns = cols[:, 0:1] * point_rows[0:1] + cols[:, 1:2] * point_rows[1:2]
        turns = turns + cols[:, 2:3] * point_rows[2:3]
        cosine, sine = turned(turns)
        phases[pl.ds(base, chunk), :] = cosine.astype(jnp.bfloat16)
        phases[pl.ds(base + chunk, chunk), :] = sine.astype(jnp.bfloat16)
        block = phases[pl.ds(base, 2 * chunk), :]
        return jnp.dot(
            block[:, 0:rows], values[1], preferred_element_type=jnp.float32
        ) + jnp.dot(
            block[:, rows : 2 * rows], values[2 - 2 * w], preferred_element_type=jnp.float32
        )

    first = True
    low_copies = {}
    for step in range(1, low_count):
        for e in order:
            index = ((high + e) % high_count) * low_count + (low + step) % low_count
            if first:
                pair_copy.wait_recv()
                first = False
            low_out[step - 1, e] = chunk_sums(index).astype(jnp.bfloat16)
            low_copies[step, e] = remote(
                low_out.at[step - 1, e],
                low_in.at[step - 1, e],
                low_send.at[step - 1, e],
                low_recv.at[step - 1, e],
                low_peer(step),
            )
            started.append(low_copies[step, e])
    for e in order:
        own_sums[e] = chunk_sums(((high + e) % high_count) * low_count + low)

    for load in loads[5:]:
        load.wait()
    turns = dist[...] * (0.5 / radius_cut)
    part = turns - jnp.floor(turns + 0.5)
    envelope[...] = (0.5 * horner(part * part, cos_terms) + 0.5) * mask[...].astype(jnp.float32)
    near[...] = jnp.zeros_like(near)
    other_copy.wait_recv()
    sharp = math.sqrt(0.5 * math.log2(math.e)) * (radial_count - 1) / radius_cut
    shift = radius_cut / (radial_count - 1)

    def near_pair(k2, carry):
        for half in range(2):
            k = k2 * 2 + half
            offset = (dist[...] - k.astype(jnp.float32) * shift) * sharp
            tiles[half * rows : (half + 1) * rows, :] = (
                jnp.exp2(-(offset * offset)) * envelope[...]
            ).astype(jnp.bfloat16)
        beside = values[...].reshape(3 * rows, values.shape[2])
        products = jnp.dot(tiles[...], beside, preferred_element_type=jnp.float32)
        near[...] += (
            products[0:rows] * filter_short[pl.ds(k2 * 2, 1), :]
            + products[rows : 2 * rows] * filter_short[pl.ds(k2 * 2 + 1, 1), :]
        )
        return carry

    pairs = radial_count // 2
    done = 0

    def near_until(stop):
        nonlocal done
        if stop > done:
            lax.fori_loop(done, stop, near_pair, 0)
            done = stop

    high_copies = {}
    for place, e in enumerate(order):
        near_until(min(pairs, place + 1))
        total = own_sums[e]
        for step in range(1, low_count):
            low_copies[step, e].wait_recv()
            total = total + low_in[step - 1, e].astype(jnp.float32)
        if e == 0:
            own_sums[0] = total
        else:
            high_out[e - 1] = total.astype(jnp.bfloat16)
            high_copies[e] = remote(
                high_out.at[e - 1],
                high_in.at[e - 1],
                high_send.at[e - 1],
                high_recv.at[e - 1],
                high_peer(e),
            )
            started.append(high_copies[e])

    near_until(min(pairs, high_count + 2))
    total = own_sums[0]
    for e in range(1, high_count):
        high_copies[e].wait_recv()
        total = total + high_in[e - 1].astype(jnp.float32)
    own_filter = block_filter[pl.ds(pl.multiple_of(a * chunk, chunk), chunk), :]

    def chunk_rows(index):
        return pl.ds(pl.multiple_of(index * 2 * chunk, 2 * chunk), 2 * chunk)

    own_rows = chunk_rows(a)
    filtered[own_rows, :] = (total * jnp.concatenate([own_filter, own_filter], axis=0)).astype(
        jnp.bfloat16
    )
    spread = {}
    for e in order:
        if e:
            spread[e] = remote(
                filtered.at[own_rows],
                filtered.at[own_rows],
                spread_send.at[e - 1],
                spread_recv.at[e - 1],
                high_peer(e),
            )
            started.append(spread[e])
    relay = []

    def pass_on(e):
        source = ((high - e + high_count) % high_count) * low_count + low
        for step in range(1, low_count):
            copy = remote(
                filtered.at[chunk_rows(source)],
                filtered.at[chunk_rows(source)],
                relay_send.at[step - 1, e],
                relay_recv.at[step - 1, e],
                low_peer(step),
            )
            relay.append(copy)
            started.append(copy)

    pass_on(0)
    near_until(pairs)
    phases_t[...] = phases[...].T
    for e in sorted(range(1, high_count), key=lambda e: -abs(2 * e - high_count)):
        spread[e].wait_recv()
        pass_on(e)
    for copy in relay:
        copy.wait_recv()

    far_out[...] = jnp.dot(
        phases_t[rows : 2 * rows, :], filtered[...], preferred_element_type=jnp.float32
    ).astype(jnp.bfloat16)
    far_copy = remote(far_out, far_in, pair_send.at[3], pair_recv.at[3], partner)
    started.append(far_copy)
    own_far = jnp.dot(phases_t[0:rows, :], filtered[...], preferred_element_type=jnp.float32)
    combined = features[...].astype(jnp.float32) + near[...]
    far_copy.wait_recv()
    far_field = (own_far + far_in[...].astype(jnp.float32)) * (float(2 * wave_count) ** -0.5)
    combined = combined + far_field
    normed = (
        combined
        * lax.rsqrt(jnp.mean(combined * combined, axis=-1, keepdims=True) + 1e-06)
        * gain[...]
    ).astype(jnp.bfloat16)
    inner = jnp.dot(normed, w_inner[...], preferred_element_type=jnp.float32)
    inner = (inner / (1.0 + jnp.exp(-inner))).astype(jnp.bfloat16)
    result = jnp.dot(inner, w_outer[...], preferred_element_type=jnp.float32) * occupied
    updated[...] = result.astype(jnp.bfloat16)
    for copy in started:
        copy.wait_send()


def kernel_body(low_count, high_count, features, positions, distances, pair_mask, counts,
                wave_index, w_value, filter_short, filter_long, gain, w_inner, w_outer):
    rows, width = features.shape
    wave_count = wave_index.shape[1]
    atoms_count = low_count * high_count
    chunk2 = 2 * wave_count // atoms_count
    columns = distances.shape[1]
    bf16, f32 = jnp.bfloat16, jnp.float32
    vmem = pl.BlockSpec(memory_space=pltpu.VMEM)
    hbm = pl.BlockSpec(memory_space=pltpu.HBM)
    smem = pl.BlockSpec(memory_space=pltpu.SMEM)
    dma = pltpu.SemaphoreType.DMA
    return pl.pallas_call(
        functools.partial(kernel, low_count, high_count),
        out_shape=jax.ShapeDtypeStruct((rows, width), bf16),
        in_specs=[hbm] * 4 + [smem] + [hbm] * 7,
        out_specs=vmem,
        scratch_shapes=[
            pltpu.VMEM((rows, width), bf16),
            pltpu.VMEM((rows, columns), f32),
            pltpu.VMEM((rows, columns), jnp.int32),
            pltpu.VMEM(wave_index.shape, jnp.int32),
            pltpu.VMEM(w_value.shape, bf16),
            pltpu.VMEM(filter_short.shape, f32),
            pltpu.VMEM(filter_long.shape, f32),
            pltpu.VMEM((1, width), f32),
            pltpu.VMEM(w_inner.shape, bf16),
            pltpu.VMEM(w_outer.shape, bf16),
            pltpu.VMEM((3, rows, width), bf16),
            pltpu.VMEM((2, 3, rows), f32),
            pltpu.VMEM((8, wave_count), f32),
            pltpu.VMEM((wave_count, 8), f32),
            pltpu.VMEM((2 * wave_count, 2 * rows), bf16),
            pltpu.VMEM((2 * rows, 2 * wave_count), bf16),
            pltpu.VMEM((high_count, chunk2, width), f32),
            pltpu.VMEM((low_count - 1, high_count, chunk2, width), bf16),
            pltpu.VMEM((low_count - 1, high_count, chunk2, width), bf16),
            pltpu.VMEM((high_count - 1, chunk2, width), bf16),
            pltpu.VMEM((high_count - 1, chunk2, width), bf16),
            pltpu.VMEM((2 * wave_count, width), bf16),
            pltpu.VMEM((wave_count, width), f32),
            pltpu.VMEM((rows, columns), f32),
            pltpu.VMEM((2 * rows, columns), bf16),
            pltpu.VMEM((rows, width), f32),
            pltpu.VMEM((rows, width), bf16),
            pltpu.VMEM((rows, width), bf16),
            dma((11,)),
            dma((4,)),
            dma((4,)),
            dma((low_count - 1, high_count)),
            dma((low_count - 1, high_count)),
            dma((high_count - 1,)),
            dma((high_count - 1,)),
            dma((high_count - 1,)),
            dma((high_count - 1,)),
            dma((low_count - 1, high_count)),
            dma((low_count - 1, high_count)),
        ],
        compiler_params=pltpu.CompilerParams(
            collective_id=0, has_side_effects=True, vmem_limit_bytes=63 * 1024 * 1024
        ),
        cost_estimate=pl.CostEstimate(
            flops=2 * rows * columns * width * filter_short.shape[0],
            bytes_accessed=8 * rows * columns,
            transcendentals=rows * columns * filter_short.shape[0],
        ),
    )(features, positions, distances, pair_mask, counts, wave_index, w_value, filter_short,
      filter_long, gain.reshape(1, width), w_inner, w_outer)


def body_for(mesh):
    atoms_count = mesh.shape["atoms"]
    low_count, high_count = split_of(atoms_count)

    def body(*arrays):
        chunk = arrays[5].shape[1] // atoms_count
        if low_count > 1 and chunk % 16 == 0 and arrays[5].shape[1] % atoms_count == 0:
            return kernel_body(low_count, high_count, *arrays)
        return collective_body(*arrays)

    return body


def solution(mesh):
    placed = (
        P(("groups", "atoms", "waves"), None),
        P(None, ("groups", "atoms", "waves")),
        P(("groups", "atoms", "waves"), None),
        P(("groups", "atoms", "waves"), None),
        P(("groups", "atoms", "waves")),
        P(None, ("groups", "waves")),
        P(),
        P(),
        P(),
        P(),
        P(),
        P(),
    )
    return jax.shard_map(
        body_for(mesh),
        mesh=mesh,
        in_specs=placed,
        out_specs=P(("groups", "atoms", "waves"), None),
        check_vma=False,
    )
```
